256 devices in a mesh: pa: 16 (over x, z_lo), pb: 16 (over z_hi, y, core).
Axes of the slice: x: 4, y: 4, z: 8 (z_hi: 2, z_lo: 4; z = z_hi * 4 + z_lo), core: 2. Of those that a mesh axis runs over, the one named last changes fastest.
Arguments:
- amplitudes: bfloat16 [384, 384, 2, 384], P('pa', 'pb'), may hold values from -6 to 6
- prev_slope: bfloat16 [384, 384, 2, 384], P('pa', 'pb'), may hold values from -6 to 6
- cholesky_vectors: bfloat16 [2304, 384, 384], P('pb', 'pa'), may hold values from -0.0625 to 0.0625
- energies: float32 [384], replicated, may hold values from -2 to 2
- occupations: float32 [384], replicated, may hold values from 0.02 to 0.98
Outputs:
- section_slope: bfloat16 [384, 384, 2, 384], P('pa', 'pb')
The draws below stay inside these ranges and needn't reach their ends.
All inputs are finite; a program needn't handle non-finite values.
Results may differ from the reference program's by a relative error of at most 0.0063.
Values may be sent and summed in bfloat16 or wider, within the bound.
A program may use at most 128 MiB of HBM per device.

```python
import jax
import jax.numpy as jnp

N = 384
L = 2304
R = 2


def level_of(key, extent, split, least, largest):
    def one(axis_at, blocks):
        draws = jax.random.uniform(jax.random.fold_in(jax.random.fold_in(key, 6), axis_at), (blocks,), jnp.float32, least / len(split), largest / len(split))
        return jnp.repeat(jnp.exp(draws), extent[axis_at] // blocks).reshape((-1,) + (1,) * (len(extent) - axis_at - 1))

    loudness = one(*split[0])
    for cut in split[1:]:
        loudness = loudness * one(*cut)
    return loudness


def normal_values(key, extent, scale, reach, split=(), dtype=jnp.bfloat16):
    entries = scale * jax.random.normal(key, extent, jnp.float32)
    if split:
        entries = entries * level_of(key, extent, split, -0.22, 0.18)
    return jnp.clip(entries, -reach, reach).astype(dtype)


def setup_inputs(seed: int = 0) -> dict:
    arg_keys = jax.random.split(jax.random.key(seed), 6)
    return {
        "amplitudes": normal_values(arg_keys[0], (N, N, R, N), 1.0, 6.0, ((0, 16), (1, 16))),
        "prev_slope": normal_values(arg_keys[1], (N, N, R, N), 1.0, 6.0, ((0, 16), (1, 16))),
        "cholesky_vectors": normal_values(arg_keys[2], (L, N, N), (N * max(4, L // 85)) ** -0.5, 0.0625, ((0, 16), (1, 16))),
        "energies": jnp.clip(jax.random.uniform(arg_keys[3], (N,), jnp.float32, -2.0, 2.0), -2.0, 2.0),
        "occupations": jnp.clip(jax.random.uniform(arg_keys[4], (N,), jnp.float32, 0.02, 0.98), 0.02, 0.98),
    }


def reference(amplitudes, prev_slope, cholesky_vectors, energies, occupations):
    hole_weight = 1.0 - 2.0 * occupations
    weighted = (cholesky_vectors.astype(jnp.float32) * hole_weight[None, :, None]).astype(jnp.bfloat16)
    exchange = jnp.dot(weighted.reshape(-1, N).T, cholesky_vectors.reshape(-1, N), preferred_element_type=jnp.float32)
    fock_matrix = (jnp.diag(energies) - exchange).astype(jnp.bfloat16)
    section_amps = (amplitudes.astype(jnp.float32) + 0.5 * prev_slope.astype(jnp.float32)).astype(jnp.bfloat16)
    antisym = (section_amps.astype(jnp.float32) - jnp.swapaxes(section_amps, 0, 1).astype(jnp.float32)).astype(jnp.bfloat16)
    left_term = jnp.dot(fock_matrix, antisym.reshape(N, -1), preferred_element_type=jnp.float32).reshape(N, N, R, N)
    reordered = jnp.transpose(antisym, (0, 2, 3, 1)).reshape(-1, N)
    right_flat = jnp.dot(reordered, fock_matrix.T, preferred_element_type=jnp.float32).reshape(N, R, N, N)
    right_term = jnp.transpose(right_flat, (0, 3, 1, 2))
    factor = 1.0 - occupations[:, None] - occupations[None, :]
    return (-(factor[:, :, None, None]) * (left_term + right_term)).astype(jnp.bfloat16)
```

```python
import functools

import jax
import jax.numpy as jnp
from jax import lax
from jax.experimental import pallas as pl
from jax.experimental.pallas import tpu as pltpu
from jax.sharding import PartitionSpec as P

N = 384
B = 24
K = 3


def place(j):
    pa = lax.axis_index("pa")
    pb = lax.axis_index("pb")
    x, y, z, c = pa // 4, (pb // 2) % 4, (pb // 8) * 4 + pa % 4, pb % 2
    dc, dz, dy, dx = j % 2, (j // 2) % 8, (j // 16) % 4, j // 64
    x, y, z, c = (x + dx) % 4, (y + dy) % 4, (z + dz) % 8, (c + dc) % 2
    return x * 4 + z % 4, (z // 4) * 8 + y * 2 + c


def exchange_kernel(spread, x_ref, o_ref, send, recv):
    me = lax.axis_index("pa") * 16 + lax.axis_index("pb")

    def step(j, _):
        qa, qb = place(j)
        source = x_ref.at[qa * 16 + qb] if spread else x_ref.at[0]
        pltpu.make_async_remote_copy(
            source, o_ref.at[me], send, recv, device_id=(qa, qb), device_id_type=pl.DeviceIdType.MESH
        ).start()
        return 0

    lax.fori_loop(1, 256, step, 0)
    o_ref[me] = x_ref[me] if spread else x_ref[0]
    part = o_ref.at[pl.ds(0, 255)]
    pltpu.make_async_copy(part, part, send).wait()
    pltpu.make_async_copy(part, part, recv).wait()


def exchange(x, spread=True):
    return pl.pallas_call(
        functools.partial(exchange_kernel, spread),
        out_shape=jax.ShapeDtypeStruct((256,) + x.shape[1:], x.dtype),
        in_specs=[pl.BlockSpec(memory_space=pltpu.VMEM)],
        out_specs=pl.BlockSpec(memory_space=pltpu.VMEM),
        scratch_shapes=[pltpu.SemaphoreType.DMA, pltpu.SemaphoreType.DMA],
        compiler_params=pltpu.CompilerParams(has_side_effects=True, vmem_limit_bytes=40 << 20),
    )(x)


def shards(amplitudes, prev_slope, cholesky_vectors, energies, occupations):
    pa, pb = lax.axis_index("pa"), lax.axis_index("pb")
    section = (amplitudes.astype(jnp.float32) + 0.5 * prev_slope.astype(jnp.float32)).astype(jnp.bfloat16)
    send = section.reshape(B * B, 256, K).transpose(1, 2, 0).reshape(256, K * B * B)
    send = jnp.pad(send, ((0, 0), (0, 2048 - K * B * B))).reshape(256, 16, 128)
    got = exchange(send).reshape(256, 2048)[:, : K * B * B]

    local_occ = lax.dynamic_slice_in_dim(occupations, pa * B, B)
    weighted = (cholesky_vectors.astype(jnp.float32) * (1.0 - 2.0 * local_occ)[None, :, None]).astype(jnp.bfloat16)
    partial = lax.dot_general(
        weighted, cholesky_vectors, (((0, 1), (0, 1)), ((), ())), preferred_element_type=jnp.float32
    )
    partial = jnp.pad(partial.reshape(256, 576), ((0, 0), (0, 448))).reshape(256, 8, 128)
    mine = exchange(partial).sum(axis=0, keepdims=True)
    total = exchange(mine, spread=False).reshape(256, 1024)[:, :576].reshape(N, N)
    fock = (jnp.diag(energies) - total).astype(jnp.bfloat16)

    s = got.reshape(16, 16, K, B, B).transpose(2, 0, 3, 1, 4).reshape(K, N, N)
    anti = (s.astype(jnp.float32) - jnp.swapaxes(s, 1, 2).astype(jnp.float32)).astype(jnp.bfloat16)
    left = jnp.einsum("pt,ktq->kpq", fock, anti, preferred_element_type=jnp.float32)
    right = jnp.einsum("kpu,qu->kpq", anti, fock, preferred_element_type=jnp.float32)
    factor = 1.0 - occupations[:, None] - occupations[None, :]
    out = (-factor[None] * (left + right)).astype(jnp.bfloat16)
    out = out.reshape(K, 16, B, 16, B).transpose(1, 3, 0, 2, 4).reshape(256, K * B * B)
    out = jnp.pad(out, ((0, 0), (0, 2048 - K * B * B))).reshape(256, 16, 128)
    back = exchange(out).reshape(256, 2048)[:, : K * B * B].reshape(768, B * B)
    return back.T.reshape(B, B, 2, N)


def solution(mesh):
    in_specs = (P("pa", "pb", None, None), P("pa", "pb", None, None), P("pb", "pa", None), P(), P())
    out_specs = P("pa", "pb", None, None)
    return jax.shard_map(shards, mesh=mesh, in_specs=in_specs, out_specs=out_specs, check_vma=False)
```

```python
import functools

import jax
import jax.numpy as jnp
from jax import lax
from jax.experimental import pallas as pl
from jax.experimental.pallas import tpu as pltpu
from jax.sharding import PartitionSpec as P

N = 384
B = 24
K = 3
BB = B * B
D = 256
F32 = jnp.float32
BF16 = jnp.bfloat16
MESH = pl.DeviceIdType.MESH


def place():
    pa = lax.axis_index("pa")
    pb = lax.axis_index("pb")
    return pa // 4, (pb // 2) % 4, (pb // 8) * 4 + pa % 4, pb % 2


def device(x, y, z, c):
    return x * 4 + z % 4, (z // 4) * 8 + y * 2 + c


def partner(j):
    x, y, z, c = place()
    dc, dz, dy, dx = j % 2, (j // 2) % 8, (j // 16) % 4, j // 64
    return device((x + dx) % 4, (y + dy) % 4, (z + dz) % 8, (c + dc) % 2)


def iota(shape, axis):
    return lax.broadcasted_iota(jnp.int32, shape, axis)


def one_hot(mask):
    return jnp.where(mask, 1.0, 0.0).astype(BF16)


def dot(a, b):
    return jnp.dot(a, b, preferred_element_type=F32)


def dot_t(a, b):
    return lax.dot_general(a, b, (((1,), (1,)), ((), ())), preferred_element_type=F32)


def pack(z, mix, buf):
    for u in range(7):
        pair = jnp.concatenate(
            [z[256 * u : 256 * u + 128, :], z[256 * u + 128 : 256 * u + 256, :]], axis=1
        ).astype(BF16)
        rows = dot_t(mix[...], pair).astype(BF16)
        buf[:, u] = rows.reshape(D, 2, 128)


def unpack(buf, mix_t, eye, z):
    for u in range(7):
        rows = buf[:, u].reshape(2 * D, 128)
        parted = dot(mix_t[...], rows).astype(BF16)
        turned = dot_t(eye, parted)
        z[256 * u : 256 * u + 128, :] = turned[:, :D].astype(z.dtype)
        z[256 * u + 128 : 256 * u + 256, :] = turned[:, D:].astype(z.dtype)


def turn_blocks(xs):
    xs = list(xs)
    block = iota(xs[0].shape, 1) // 16
    for w in (1, 2, 4):
        high = (block & w) != 0
        for i in range(8):
            if i & w == 0:
                a, b = xs[i], xs[i + w]
                xs[i] = jnp.where(high, pltpu.roll(b, 16 * w, 1), a)
                xs[i + w] = jnp.where(high, b, pltpu.roll(a, 128 - 16 * w, 1))
    return xs


def kernel(amp, prev, chol, hole, energies, factor, out,
           z16, z32, mix, mix_t, send1, recv1, send2, recv2, mats, holes,
           partial, half, sums, from_core, from_y, from_z, from_x, rows48, fock, sems, rsems):
    x, y, z, c = place()
    me_a, me_b = device(x, y, z, c)
    me = me_b * 16 + me_a

    barrier = pltpu.get_barrier_semaphore()

    def greet(j, _):
        pl.semaphore_signal(barrier, inc=1, device_id=partner(j), device_id_type=MESH)
        return 0

    lax.fori_loop(1, D, greet, 0)

    def start(source, target, stage, where):
        pltpu.make_async_remote_copy(
            source, target, sems.at[stage], rsems.at[stage], device_id=where, device_id_type=MESH
        ).start()

    def wait(sem, like):
        pltpu.make_async_copy(like, like, sem).wait()

    def ship(lo, hi, source, target, stage):
        def step(j, _):
            qa, qb = partner(j)
            start(source.at[qb * 16 + qa], target.at[me], stage, (qa, qb))
            return 0

        lax.fori_loop(lo, hi, step, 0)

    r, q = iota((512, 512), 0), iota((512, 512), 1)
    mix[...] = one_hot(r // 2 + (r % 2) * D == q)
    mix_t[...] = one_hot(q // 2 + (q % 2) * D == r)
    eye = one_hot(iota((128, 128), 0) == iota((128, 128), 1))

    for i in range(0, BB, 64):
        s = amp[i : i + 64].astype(F32) + 0.5 * prev[i : i + 64].astype(F32)
        s = s.reshape(64, 2 * N).astype(BF16)
        for j in range(K):
            z16[j * BB + i : j * BB + i + 64, :] = s[:, j * D : (j + 1) * D]
    z16[K * BB :, :] = jnp.zeros((64, D), BF16)
    pack(z16, mix, send1)
    send1_own = send1[pl.ds(me, 1)]
    recv1[pl.ds(me, 1)] = send1_own

    pl.semaphore_wait(barrier, D - 1)
    ship(1, 64, send1, recv1, 0)

    for i in range(16):
        holes[i * B : (i + 1) * B, :] = hole[...]
    partial[...] = jnp.zeros((N, N), F32)

    def rank_rows(i, _):
        rows = chol[pl.ds(pl.multiple_of(i * N, N), N), :]
        weighted = (rows.astype(F32) * holes[...]).astype(BF16)
        partial[...] += lax.dot_general(
            weighted, rows, (((0,), (0,)), ((), ())), preferred_element_type=F32
        )
        return 0

    lax.fori_loop(0, 9, rank_rows, 0)

    start(partial.at[pl.ds(192 * (1 - c), 192)], from_core, 1, device(x, y, z, 1 - c))
    ship(64, 128, send1, recv1, 0)
    wait(rsems.at[1], from_core)
    half[...] = partial[pl.ds(192 * c, 192), :] + from_core[...]
    for d in (1, 2, 3):
        y2 = (y + d) % 4
        start(half.at[pl.ds(48 * y2, 48)], from_y.at[y], 2, device(x, y2, z, c))
    from_y[pl.ds(y, 1)] = half[pl.ds(48 * y, 48), :][None]
    ship(128, 176, send1, recv1, 0)
    wait(rsems.at[2], from_y.at[pl.ds(0, 3)])
    sums[...] = from_y[0] + from_y[1] + from_y[2] + from_y[3]
    for d in range(1, 8):
        z2 = (z + d) % 8

        @pl.when(z2 < 6)
        def _():
            start(sums.at[pl.ds(8 * z2, 8)], from_z.at[z], 3, device(x, y, z2, c))

    ship(176, 216, send1, recv1, 0)

    @pl.when(z < 6)
    def _():
        from_z[pl.ds(z, 1)] = sums[pl.ds(8 * z, 8), :][None]
        wait(rsems.at[3], from_z.at[pl.ds(0, 7)])
        total = from_z[0]
        for d in range(1, 8):
            total = total + from_z[d]
        from_x[pl.ds(x, 1)] = total[None]
        for d in (1, 2, 3):
            x2 = (x + d) % 4
            start(from_x.at[x], from_x.at[x], 4, device(x2, y, z, c))

    ship(216, D, send1, recv1, 0)

    @pl.when(z < 6)
    def _():
        wait(rsems.at[4], from_x.at[pl.ds(0, 3)])
        rows48[pl.ds(8 * z, 8), :] = from_x[0] + from_x[1] + from_x[2] + from_x[3]
        for d in range(1, 8):
            mine = rows48.at[pl.ds(8 * z, 8)]
            start(mine, mine, 5, device(x, y, (z + d) % 8, c))
        wait(rsems.at[5], rows48.at[pl.ds(0, 40)])

    @pl.when(z >= 6)
    def _():
        wait(rsems.at[5], rows48)

    first = 192 * c + 48 * y
    diagonal = jnp.where(iota((48, N), 0) + first == iota((48, N), 1), energies[...], 0.0)
    fock[pl.ds(pl.multiple_of(first, 48), 48), :] = (diagonal - rows48[...]).astype(BF16)
    mine = fock.at[pl.ds(pl.multiple_of(first, 48), 48)]
    for d in (1, 2, 3):
        start(mine, mine, 6, device(x, (y + d) % 4, z, c))
    wait(rsems.at[6], fock.at[pl.ds(0, 144)])
    mine = fock.at[pl.ds(pl.multiple_of(192 * c, 192), 192)]
    start(mine, mine, 7, device(x, y, z, 1 - c))
    wait(rsems.at[7], mine)

    wait(rsems.at[0], recv1.at[pl.ds(0, D - 1)])
    unpack(recv1, mix_t, eye, z32)
    for j in range(K):
        for pg in range(3):
            for bg in range(2):
                rows = [j * BB + (pg * 8 + i) * B for i in range(8)]
                got = turn_blocks([z32[h : h + B, bg * 128 : bg * 128 + 128] for h in rows])
                for i in range(8):
                    h = (bg * 8 + i) * B
                    mats[j, h : h + B, pg * 128 : pg * 128 + 128] = got[i]

    lane, p = iota((N, N), 0), iota((N, N), 1)
    order_t = one_hot((lane % 16) * B + lane // 16 == p)
    order = one_hot((p % 16) * B + p // 16 == lane)
    for j in range(K):
        held = mats[j].astype(BF16)
        anti = (dot_t(order, held) - dot(held, order_t)).astype(BF16)
        both = dot(fock[...], anti) + dot_t(anti, fock[...])
        slope = (factor[...] * both).astype(BF16)
        mats[j] = dot(slope, order)
        for pg in range(3):
            for bg in range(2):
                rows = [(bg * 8 + i) * B for i in range(8)]
                got = turn_blocks([mats[j, h : h + B, pg * 128 : pg * 128 + 128] for h in rows])
                for i in range(8):
                    h = j * BB + (pg * 8 + i) * B
                    z32[h : h + B, bg * 128 : bg * 128 + 128] = got[i]
    pack(z32, mix, send2)
    recv2[pl.ds(me, 1)] = send2[pl.ds(me, 1)]
    ship(1, D, send2, recv2, 8)
    wait(rsems.at[8], recv2.at[pl.ds(0, D - 1)])
    unpack(recv2, mix_t, eye, z16)
    for i in range(0, BB, 64):
        s = jnp.concatenate([z16[j * BB + i : j * BB + i + 64, :] for j in range(K)], axis=1)
        out[i : i + 64] = s.reshape(64, 2, N)

    wait(sems.at[0], send1.at[pl.ds(0, D - 1)])
    wait(sems.at[1], from_core)
    wait(sems.at[2], from_y.at[pl.ds(0, 3)])

    @pl.when(z < 6)
    def _():
        wait(sems.at[3], from_z.at[pl.ds(0, 5)])
        wait(sems.at[4], from_x.at[pl.ds(0, 3)])
        wait(sems.at[5], from_z.at[pl.ds(0, 7)])

    @pl.when(z >= 6)
    def _():
        wait(sems.at[3], from_z.at[pl.ds(0, 6)])

    wait(sems.at[6], fock.at[pl.ds(0, 144)])
    wait(sems.at[7], fock.at[pl.ds(0, 192)])
    wait(sems.at[8], send2.at[pl.ds(0, D - 1)])


def shards(amplitudes, prev_slope, cholesky_vectors, energies, occupations):
    pa = lax.axis_index("pa")
    local_occ = lax.dynamic_slice_in_dim(occupations, pa * B, B)
    hole = jnp.broadcast_to((1.0 - 2.0 * local_occ)[:, None], (B, N))
    factor = 1.0 - occupations[:, None] - occupations[None, :]
    vmem = pl.BlockSpec(memory_space=pltpu.VMEM)
    slope = pl.pallas_call(
        kernel,
        out_shape=jax.ShapeDtypeStruct((BB, 2, N), BF16),
        in_specs=[vmem] * 6,
        out_specs=vmem,
        scratch_shapes=[
            pltpu.VMEM((1792, D), BF16),
            pltpu.VMEM((1792, D), F32),
            pltpu.VMEM((512, 512), BF16),
            pltpu.VMEM((512, 512), BF16),
            pltpu.VMEM((D, 7, 2, 128), BF16),
            pltpu.VMEM((D, 7, 2, 128), BF16),
            pltpu.VMEM((D, 7, 2, 128), BF16),
            pltpu.VMEM((D, 7, 2, 128), BF16),
            pltpu.VMEM((K, N, N), F32),
            pltpu.VMEM((N, N), F32),
            pltpu.VMEM((N, N), F32),
            pltpu.VMEM((192, N), F32),
            pltpu.VMEM((48, N), F32),
            pltpu.VMEM((192, N), F32),
            pltpu.VMEM((4, 48, N), F32),
            pltpu.VMEM((8, 8, N), F32),
            pltpu.VMEM((4, 8, N), F32),
            pltpu.VMEM((48, N), F32),
            pltpu.VMEM((N, N), BF16),
            pltpu.SemaphoreType.DMA((9,)),
            pltpu.SemaphoreType.DMA((9,)),
        ],
        compiler_params=pltpu.CompilerParams(
            collective_id=0, has_side_effects=True, vmem_limit_bytes=56 << 20
        ),
    )(
        amplitudes.reshape(BB, 2, N),
        prev_slope.reshape(BB, 2, N),
        cholesky_vectors.reshape(-1, N),
        hole,
        energies.reshape(1, N),
        factor,
    )
    return slope.reshape(B, B, 2, N)


def solution(mesh):
    in_specs = (P("pa", "pb", None, None), P("pa", "pb", None, None), P("pb", "pa", None), P(), P())
    out_specs = P("pa", "pb", None, None)
    return jax.shard_map(shards, mesh=mesh, in_specs=in_specs, out_specs=out_specs, check_vma=False)
```

```python
import jax
import jax.numpy as jnp
from jax import lax
from jax.experimental import pallas as pl
from jax.experimental.pallas import tpu as pltpu
from jax.sharding import PartitionSpec as P

N = 384
B = 24
K = 3
BB = B * B
D = 256
UNITS = 7
F32 = jnp.float32
BF16 = jnp.bfloat16
MESH = pl.DeviceIdType.MESH
IN_PARTS = ((0, 3), (3, 2), (5, 2))
OUT_PARTS = ((0, 2), (2, 2), (4, 3))


def place():
    pa = lax.axis_index("pa")
    pb = lax.axis_index("pb")
    return pa >> 2, (pb >> 1) & 3, ((pb >> 3) << 2) | (pa & 3), pb & 1


def device(x, y, z, c):
    return (x << 2) | (z & 3), ((z >> 2) << 3) | (y << 1) | c


def partner(j):
    x, y, z, c = place()
    return device((x + (j >> 6)) & 3, (y + ((j >> 4) & 3)) & 3, (z + ((j >> 1) & 7)) & 7, (c + j) & 1)


def iota(shape, axis):
    return lax.broadcasted_iota(jnp.int32, shape, axis)


def one_hot(mask):
    return jnp.where(mask, 1.0, 0.0).astype(BF16)


def dot(a, b):
    return jnp.dot(a, b, preferred_element_type=F32)


def dot_t(a, b):
    return lax.dot_general(a, b, (((1,), (1,)), ((), ())), preferred_element_type=F32)


def row_home(rho):
    return ((rho >> 1) & 15) * B + (rho >> 5) * 2 + (rho & 1)


def lane_home(kappa):
    return ((kappa >> 3) & 15) * B + (kappa >> 7) * 8 + (kappa & 7)


def turn_blocks(xs, lane):
    xs = list(xs)
    for w in (1, 2, 4, 8):
        high = (lane & (8 * w)) != 0
        for i in range(16):
            if i & w == 0:
                a, b = xs[i], xs[i + w]
                xs[i] = jnp.where(high, pltpu.roll(b, 8 * w, 1), a)
                xs[i + w] = jnp.where(high, b, pltpu.roll(a, 128 - 8 * w, 1))
    return xs


def kernel(amp_hbm, prev_hbm, chol_hbm, energies, occ, out,
           amp, prev, chol, zs, mix, mix_t, send1, recv1, send2, recv2, mats, outs, holes,
           partial, half, sums, from_core, from_y, from_z, from_x, rows48, fock, fock_p, factor, turn, turn_t,
           greet, loads, sems, rsems):
    x, y, z, c = place()
    me_a, me_b = device(x, y, z, c)
    me = (me_b << 4) | me_a

    load_amp = pltpu.make_async_copy(amp_hbm, amp, loads.at[0])
    load_prev = pltpu.make_async_copy(prev_hbm, prev, loads.at[1])
    load_chol = pltpu.make_async_copy(chol_hbm, chol, loads.at[2])
    load_amp.start()
    load_prev.start()
    load_chol.start()

    barrier = pltpu.get_barrier_semaphore()
    column = [device(x, y, (z + d) & 7, c ^ e) for d in range(8) for e in range(2) if d or e]
    plane = [device((x + d) & 3, (y + e) & 3, z, c) for d in range(4) for e in range(4) if d or e]
    for where in column + plane:
        pl.semaphore_signal(barrier, inc=1, device_id=where, device_id_type=MESH)

    def start(source, target, stage, where):
        pltpu.make_async_remote_copy(
            source, target, sems.at[stage], rsems.at[stage], device_id=where, device_id_type=MESH
        ).start()

    def wait(sem, like):
        pltpu.make_async_copy(like, like, sem).wait()

    def ship(lo, hi, part, source, target, stage):
        units = pl.ds(part[0], part[1])

        def step(j, _):
            qa, qb = partner(j)
            start(source.at[units, (qb << 4) | qa], target.at[units, me], stage, (qa, qb))
            return 0

        lax.fori_loop(lo, hi, step, 0)

    def all_but_one(buf, part):
        return buf.at[pl.ds(part[0], part[1]), pl.ds(0, D - 1)]

    r, q = iota((512, 512), 0), iota((512, 512), 1)
    mix[...] = one_hot((r >> 1) + (r & 1) * D == q)
    mix_t[...] = one_hot((q >> 1) + (q & 1) * D == r)
    eye = one_hot(iota((128, 128), 0) == iota((128, 128), 1))

    load_amp.wait()
    load_prev.wait()
    for h in range(0, BB, 3 * B):
        s = amp[h : h + 3 * B].astype(F32) + 0.5 * prev[h : h + 3 * B].astype(F32)
        s = s.reshape(3 * B, 2 * N)
        for t in range(0, 3 * B, 8):
            p, g = (h + t) // B, ((h + t) % B) // 8
            for j in range(K):
                at = ((j * 3 + g) * 12 + p // 2) * 8
                zs[p % 2, at : at + 8, :] = s[t : t + 8, j * D : (j + 1) * D]
    for i in range(2):
        zs[i, 3 * BB // 2 :, :] = jnp.zeros((32, D), F32)
    folded = send1.reshape(UNITS, 2 * D, 128)
    for u in range(UNITS):
        pair = jnp.concatenate([zs[i, 128 * u : 128 * u + 128, :] for i in range(2)], axis=1).astype(BF16)
        folded[u] = dot_t(mix[...], pair).astype(BF16)
    recv1[:, pl.ds(me, 1)] = send1[:, pl.ds(me, 1)]

    pl.semaphore_wait(barrier, len(column + plane))
    for where in plane:
        pl.semaphore_signal(greet, inc=1, device_id=where, device_id_type=MESH)
    pl.semaphore_wait(greet, len(plane))
    ship(1, D, IN_PARTS[0], send1, recv1, 0)

    spread = jnp.broadcast_to(occ[...], (128, N))
    upright = jnp.transpose(spread)
    partial[:, 0:128] = upright
    hole = 1.0 - 2.0 * partial[pl.ds(pl.multiple_of(me_a * B, 8), B), 0:128]
    for i in range(16):
        for t in range(3):
            holes[i * B : (i + 1) * B, t * 128 : t * 128 + 128] = hole
    load_chol.wait()
    partial[...] = jnp.zeros((N, N), F32)

    def rank_rows(i, _):
        rows = chol[pl.ds(pl.multiple_of(i * N, N), N), :]
        weighted = (rows.astype(F32) * holes[...]).astype(BF16)
        partial[...] += lax.dot_general(
            weighted, rows, (((0,), (0,)), ((), ())), preferred_element_type=F32
        )
        return 0

    lax.fori_loop(0, 9, rank_rows, 0)

    start(partial.at[pl.ds(192 * (1 - c), 192)], from_core, 6, device(x, y, z, 1 - c))
    ship(1, 64, IN_PARTS[1], send1, recv1, 1)
    wait(rsems.at[6], from_core)
    half[...] = partial[pl.ds(192 * c, 192), :] + from_core[...]
    for d in (1, 2, 3):
        y2 = (y + d) & 3
        start(half.at[pl.ds(48 * y2, 48)], from_y.at[y], 7, device(x, y2, z, c))
    from_y[pl.ds(y, 1)] = half[pl.ds(48 * y, 48), :][None]
    ship(64, 192, IN_PARTS[1], send1, recv1, 1)
    wait(rsems.at[7], from_y.at[pl.ds(0, 3)])
    sums[...] = from_y[0] + from_y[1] + from_y[2] + from_y[3]
    for d in range(1, 8):
        z2 = (z + d) & 7

        @pl.when(z2 < 6)
        def _():
            start(sums.at[pl.ds(8 * z2, 8)], from_z.at[z], 8, device(x, y, z2, c))

    ship(192, D, IN_PARTS[1], send1, recv1, 1)

    @pl.when(z < 6)
    def _():
        from_z[pl.ds(z, 1)] = sums[pl.ds(8 * z, 8), :][None]
        wait(rsems.at[8], from_z.at[pl.ds(0, 7)])
        total = from_z[0]
        for d in range(1, 8):
            total = total + from_z[d]
        from_x[pl.ds(x, 1)] = total[None]
        for d in (1, 2, 3):
            start(from_x.at[x], from_x.at[x], 9, device((x + d) & 3, y, z, c))

    ship(1, 64, IN_PARTS[2], send1, recv1, 2)

    @pl.when(z < 6)
    def _():
        wait(rsems.at[9], from_x.at[pl.ds(0, 3)])
        rows48[pl.ds(8 * z, 8), :] = from_x[0] + from_x[1] + from_x[2] + from_x[3]
        for d in range(1, 8):
            mine = rows48.at[pl.ds(8 * z, 8)]
            start(mine, mine, 10, device(x, y, (z + d) & 7, c))

    ship(64, 128, IN_PARTS[2], send1, recv1, 2)

    @pl.when(z < 6)
    def _():
        wait(rsems.at[10], rows48.at[pl.ds(0, 40)])

    @pl.when(z >= 6)
    def _():
        wait(rsems.at[10], rows48)

    first = 192 * c + 48 * y
    diagonal = jnp.where(iota((48, N), 0) + first == iota((48, N), 1), jnp.broadcast_to(energies[...], (48, N)), 0.0)
    fock[pl.ds(pl.multiple_of(first, 48), 48), :] = (diagonal - rows48[...]).astype(BF16)
    mine = fock.at[pl.ds(pl.multiple_of(first, 48), 48)]
    for d in (1, 2, 3):
        start(mine, mine, 11, device(x, (y + d) & 3, z, c))
    ship(128, D, IN_PARTS[2], send1, recv1, 2)

    rho, nat = iota((N, N), 0), iota((N, N), 1)
    home = row_home(rho)
    gather = one_hot(home == nat)
    turn_t[...] = one_hot(home == lane_home(nat))
    turn[...] = one_hot(lane_home(rho) == row_home(nat))
    left = spread
    order = jnp.zeros((128, N), F32)
    for _ in range(3):
        piece = left.astype(BF16)
        left = left - piece.astype(F32)
        order = order + dot_t(piece, gather)
    upright = jnp.transpose(order)
    for t in range(3):
        lanes = slice(t * 128, t * 128 + 128)
        factor[:, lanes] = -(1.0 - upright - order[0:1, lanes])

    wait(rsems.at[11], fock.at[pl.ds(0, 144)])
    mine = fock.at[pl.ds(pl.multiple_of(192 * c, 192), 192)]
    start(mine, mine, 12, device(x, y, z, 1 - c))
    wait(rsems.at[12], mine)
    fock_p[...] = dot_t(dot(gather, fock[...]).astype(BF16), gather).astype(BF16)

    block = lax.broadcasted_iota(jnp.int16, (32, 128), 1)
    taken = recv1.reshape(UNITS, 2 * D, 128)
    given = send2.reshape(UNITS, 2 * D, 128)

    def spot(u, i):
        g = 16 * u + i
        return g // 36, g % 12 * 32, g // 12 % 3 * 128

    for j in range(K):
        wait(rsems.at[j], all_but_one(recv1, IN_PARTS[j]))
        for u in range(IN_PARTS[j][0], IN_PARTS[j][0] + IN_PARTS[j][1]):
            got = turn_blocks([taken[u, 32 * b : 32 * b + 32, :] for b in range(16)], block)
            for i in range(16):
                k, row, lane = spot(u, i)
                if k < K:
                    mats[k, row : row + 32, lane : lane + 128] = got[i]
        held = mats[j]
        anti = (dot(held, turn[...]) - dot_t(turn_t[...], held)).astype(BF16)
        both = dot(fock_p[...], anti) + dot_t(anti, fock_p[...])
        slope = (factor[...] * both).astype(BF16)
        outs[j] = dot(slope, turn_t[...]).astype(BF16)
        for u in range(OUT_PARTS[j][0], OUT_PARTS[j][0] + OUT_PARTS[j][1]):
            pieces = []
            for i in range(16):
                k, row, lane = spot(u, i)
                pieces.append(outs[k, row : row + 32, lane : lane + 128] if k < K else jnp.zeros((32, 128), BF16))
            got = turn_blocks(pieces, block)
            for b in range(16):
                given[u, 32 * b : 32 * b + 32, :] = got[b]
        ship(1, D, OUT_PARTS[j], send2, recv2, 3 + j)
    recv2[:, pl.ds(me, 1)] = send2[:, pl.ds(me, 1)]

    taken = recv2.reshape(UNITS, 2 * D, 128)
    for j in range(K):
        wait(rsems.at[3 + j], all_but_one(recv2, OUT_PARTS[j]))
        for u in range(OUT_PARTS[j][0], OUT_PARTS[j][0] + OUT_PARTS[j][1]):
            turned = dot(dot_t(eye, taken[u]).astype(BF16), mix[...])
            for i in range(2):
                zs[i, 128 * u : 128 * u + 128, :] = turned[:, i * D : (i + 1) * D]
    for h in range(0, BB, 2 * B):
        rows = []
        for t in range(0, 2 * B, 8):
            p, g = (h + t) // B, ((h + t) % B) // 8
            pieces = []
            for j in range(K):
                at = ((j * 3 + g) * 12 + p // 2) * 8
                pieces.append(zs[p % 2, at : at + 8, :])
            rows.append(jnp.concatenate(pieces, axis=1))
        out[h : h + 2 * B] = jnp.concatenate(rows, axis=0).astype(BF16).reshape(2 * B, 2, N)

    for j in range(K):
        wait(sems.at[j], all_but_one(send1, IN_PARTS[j]))
        wait(sems.at[3 + j], all_but_one(send2, OUT_PARTS[j]))
    wait(sems.at[6], from_core)
    wait(sems.at[7], from_y.at[pl.ds(0, 3)])

    @pl.when(z < 6)
    def _():
        wait(sems.at[8], from_z.at[pl.ds(0, 5)])
        wait(sems.at[9], from_x.at[pl.ds(0, 3)])
        wait(sems.at[10], from_z.at[pl.ds(0, 7)])

    @pl.when(z >= 6)
    def _():
        wait(sems.at[8], from_z.at[pl.ds(0, 6)])

    wait(sems.at[11], fock.at[pl.ds(0, 144)])
    wait(sems.at[12], fock.at[pl.ds(0, 192)])


def shards(amplitudes, prev_slope, cholesky_vectors, energies, occupations):
    vmem = pl.BlockSpec(memory_space=pltpu.VMEM)
    whole = pl.BlockSpec(memory_space=pl.ANY)
    slope = pl.pallas_call(
        kernel,
        out_shape=jax.ShapeDtypeStruct((BB, 2, N), BF16),
        in_specs=[whole] * 3 + [vmem] * 2,
        out_specs=vmem,
        scratch_shapes=[
            pltpu.VMEM((BB, 2, N), BF16),
            pltpu.VMEM((BB, 2, N), BF16),
            pltpu.VMEM((144 * B, N), BF16),
            pltpu.VMEM((2, UNITS * 128, D), F32),
            pltpu.VMEM((512, 512), BF16),
            pltpu.VMEM((512, 512), BF16),
            pltpu.VMEM((UNITS, D, 2, 128), BF16),
            pltpu.VMEM((UNITS, D, 2, 128), BF16),
            pltpu.VMEM((UNITS, D, 2, 128), BF16),
            pltpu.VMEM((UNITS, D, 2, 128), BF16),
            pltpu.VMEM((K, N, N), BF16),
            pltpu.VMEM((K, N, N), BF16),
            pltpu.VMEM((N, N), F32),
            pltpu.VMEM((N, N), F32),
            pltpu.VMEM((192, N), F32),
            pltpu.VMEM((48, N), F32),
            pltpu.VMEM((192, N), F32),
            pltpu.VMEM((4, 48, N), F32),
            pltpu.VMEM((8, 8, N), F32),
            pltpu.VMEM((4, 8, N), F32),
            pltpu.VMEM((48, N), F32),
            pltpu.VMEM((N, N), BF16),
            pltpu.VMEM((N, N), BF16),
            pltpu.VMEM((N, N), F32),
            pltpu.VMEM((N, N), BF16),
            pltpu.VMEM((N, N), BF16),
            pltpu.SemaphoreType.REGULAR,
            pltpu.SemaphoreType.DMA((3,)),
            pltpu.SemaphoreType.DMA((13,)),
            pltpu.SemaphoreType.DMA((13,)),
        ],
        compiler_params=pltpu.CompilerParams(
            collective_id=0, has_side_effects=True, vmem_limit_bytes=56 << 20
        ),
    )(
        amplitudes.reshape(BB, 2, N),
        prev_slope.reshape(BB, 2, N),
        cholesky_vectors.reshape(-1, N),
        energies,
        occupations,
    )
    return slope.reshape(B, B, 2, N)


def solution(mesh):
    in_specs = (P("pa", "pb", None, None), P("pa", "pb", None, None), P("pb", "pa", None), P(), P())
    out_specs = P("pa", "pb", None, None)
    return jax.shard_map(shards, mesh=mesh, in_specs=in_specs, out_specs=out_specs, check_vma=False)
```

```python
import jax
import jax.numpy as jnp
from jax import lax
from jax.experimental import pallas as pl
from jax.experimental.pallas import tpu as pltpu
from jax.sharding import PartitionSpec as P

N = 384
B = 24
K = 3
BB = B * B
D = 256
UNITS = 7
F32 = jnp.float32
BF16 = jnp.bfloat16
MESH = pl.DeviceIdType.MESH
IN_PARTS = ((0, 3), (3, 2), (5, 2))
OUT_PARTS = ((0, 2), (2, 2), (4, 3))
GAPS = (255, 128, 128, 254)
TILES = 36


def place():
    pa = lax.axis_index("pa")
    pb = lax.axis_index("pb")
    return pa >> 2, (pb >> 1) & 3, ((pb >> 3) << 2) | (pa & 3), pb & 1


def device(x, y, z, c):
    return (x << 2) | (z & 3), ((z >> 2) << 3) | (y << 1) | c


def partner(j):
    x, y, z, c = place()
    return device((x + (j >> 6)) & 3, (y + ((j >> 4) & 3)) & 3, (z + ((j >> 1) & 7)) & 7, (c + j) & 1)


def iota(shape, axis):
    return lax.broadcasted_iota(jnp.int32, shape, axis)


def one_hot(mask):
    return jnp.where(mask, 1.0, 0.0).astype(BF16)


def dot(a, b):
    return jnp.dot(a, b, preferred_element_type=F32)


def dot_t(a, b):
    return lax.dot_general(a, b, (((1,), (1,)), ((), ())), preferred_element_type=F32)


def row_home(rho):
    return ((rho >> 1) & 15) * B + (rho >> 5) * 2 + (rho & 1)


def lane_home(kappa):
    return ((kappa >> 3) & 15) * B + (kappa >> 7) * 8 + (kappa & 7)


def turn_blocks(xs, lane):
    xs = list(xs)
    for w in (1, 2, 4, 8):
        high = (lane & (8 * w)) != 0
        for i in range(16):
            if i & w == 0:
                a, b = xs[i], xs[i + w]
                xs[i] = jnp.where(high, pltpu.roll(b, 8 * w, 1), a)
                xs[i + w] = jnp.where(high, b, pltpu.roll(a, 128 - 8 * w, 1))
    return xs


def kernel(amp_hbm, prev_hbm, chol_hbm, energies, occ, out,
           amp, prev, chol, zs, mix, mix_t, send1, recv1, send2, recv2, mats, outs, holes,
           partial, half, from_core, from_xy, from_z, level, fock_tiles, fock, fock_p, factor, turn, turn_t,
           greet, loads, sems, rsems):
    x, y, z, c = place()
    me_a, me_b = device(x, y, z, c)
    me = (me_b << 4) | me_a

    load_amp = pltpu.make_async_copy(amp_hbm, amp, loads.at[0])
    load_prev = pltpu.make_async_copy(prev_hbm, prev, loads.at[1])
    load_chol = pltpu.make_async_copy(chol_hbm, chol, loads.at[2])
    load_chol.start()
    load_amp.start()
    load_prev.start()

    barrier = pltpu.get_barrier_semaphore()
    column = [device(x, y, (z + d) & 7, c ^ e) for d in range(8) for e in range(2) if d or e]
    plane = [device((x + d) & 3, (y + e) & 3, z, c) for d in range(4) for e in range(4) if d or e]
    for where in column + plane:
        pl.semaphore_signal(barrier, inc=1, device_id=where, device_id_type=MESH)

    def start(source, target, stage, where):
        pltpu.make_async_remote_copy(
            source, target, sems.at[stage], rsems.at[stage], device_id=where, device_id_type=MESH
        ).start()

    def wait(sem, like):
        pltpu.make_async_copy(like, like, sem).wait()

    def ship(lo, hi, part, source, target, stage):
        units = pl.ds(part[0], part[1])

        def step(j, _):
            qa, qb = partner(j)
            start(source.at[units, (qb << 4) | qa], target.at[units, me], stage, (qa, qb))
            return 0

        lax.fori_loop(lo, hi, step, 0)

    queue = [(j, n) for j in range(K) for n in range(1, D)]
    sent = [0]

    def more(count):
        todo = queue[sent[0] : sent[0] + count]
        sent[0] += count
        for j in range(K):
            ns = [n for k, n in todo if k == j]
            if ns:
                ship(ns[0], ns[-1] + 1, IN_PARTS[j], send1, recv1, j)

    def all_but_one(buf, part):
        return buf.at[pl.ds(part[0], part[1]), pl.ds(0, D - 1)]

    r, q = iota((512, 512), 0), iota((512, 512), 1)
    mix[...] = one_hot((r >> 1) + (r & 1) * D == q)
    mix_t[...] = one_hot((q >> 1) + (q & 1) * D == r)
    eye = one_hot(iota((128, 128), 0) == iota((128, 128), 1))

    spread = jnp.broadcast_to(occ[...], (128, N))
    upright = jnp.transpose(spread)
    partial[:, 0:128] = upright
    hole = 1.0 - 2.0 * partial[pl.ds(pl.multiple_of(me_a * B, 8), B), 0:128]
    for i in range(16):
        for t in range(3):
            holes[i * B : (i + 1) * B, t * 128 : t * 128 + 128] = hole
    load_chol.wait()
    partial[...] = jnp.zeros((N, N), F32)

    def rank_rows(i, _):
        rows = chol[pl.ds(pl.multiple_of(i * 3 * N, N), 3 * N), :]
        weighted = jnp.concatenate(
            [(rows[t * N : (t + 1) * N].astype(F32) * holes[...]).astype(BF16) for t in range(3)], axis=0
        )
        partial[...] += lax.dot_general(
            weighted, rows, (((0,), (0,)), ((), ())), preferred_element_type=F32
        )
        return 0

    lax.fori_loop(0, 3, rank_rows, 0)

    pl.semaphore_wait(barrier, len(column + plane))
    for where in plane:
        pl.semaphore_signal(greet, inc=1, device_id=where, device_id_type=MESH)
    start(partial.at[pl.ds(192 * (1 - c), 192)], from_core, 6, device(x, y, z, 1 - c))
    load_amp.wait()
    load_prev.wait()
    for h in range(0, BB, 3 * B):
        s = amp[h : h + 3 * B].astype(F32) + 0.5 * prev[h : h + 3 * B].astype(F32)
        s = s.reshape(3 * B, 2 * N)
        for t in range(0, 3 * B, 8):
            p, g = (h + t) // B, ((h + t) % B) // 8
            for j in range(K):
                at = ((j * 3 + g) * 12 + p // 2) * 8
                zs[p % 2, at : at + 8, :] = s[t : t + 8, j * D : (j + 1) * D]
    for i in range(2):
        zs[i, 3 * BB // 2 :, :] = jnp.zeros((32, D), F32)
    folded = send1.reshape(UNITS, 2 * D, 128)
    for u in range(UNITS):
        pair = jnp.concatenate([zs[i, 128 * u : 128 * u + 128, :] for i in range(2)], axis=1).astype(BF16)
        folded[u] = dot_t(mix[...], pair).astype(BF16)
    recv1[:, pl.ds(me, 1)] = send1[:, pl.ds(me, 1)]

    wait(rsems.at[6], from_core)
    for t in range(TILES):
        r, lanes = t // 3 * 16, slice(t % 3 * 128, t % 3 * 128 + 128)
        half[t] = partial[pl.ds(192 * c + r, 16), lanes] + from_core[r : r + 16, lanes]
    own = (x << 2) | y

    def scatter(t, _):
        o = t & 15

        @pl.when(o != own)
        def _():
            start(half.at[t], from_xy.at[t >> 4, own], 7, device(o >> 2, o & 3, z, c))

        return 0

    lax.fori_loop(0, TILES, scatter, 0)
    pl.semaphore_wait(greet, len(plane))
    more(GAPS[0])
    rho, nat = iota((N, N), 0), iota((N, N), 1)
    home = row_home(rho)
    gather = one_hot(home == nat)
    turn_t[...] = one_hot(home == lane_home(nat))
    turn[...] = one_hot(lane_home(rho) == row_home(nat))
    left = spread
    order = jnp.zeros((128, N), F32)
    for _ in range(3):
        piece = left.astype(BF16)
        left = left - piece.astype(F32)
        order = order + dot_t(piece, gather)
    upright = jnp.transpose(order)
    for t in range(3):
        lanes = slice(t * 128, t * 128 + 128)
        factor[:, lanes] = -(1.0 - upright - order[0:1, lanes])

    more(GAPS[1])

    @pl.when(own < 4)
    def _():
        wait(rsems.at[7], from_xy.at[pl.ds(0, 3), pl.ds(0, 15)])
        from_xy[2, pl.ds(own, 1)] = half[pl.ds(32 + own, 1)]

    @pl.when(own >= 4)
    def _():
        wait(rsems.at[7], from_xy.at[pl.ds(0, 2), pl.ds(0, 15)])
        from_xy[2] = jnp.zeros((16, 16, 128), F32)

    for k in range(2):
        from_xy[k, pl.ds(own, 1)] = half[pl.ds(16 * k + own, 1)]
    for k in range(3):
        total = from_xy[k, 0]
        for n in range(1, 16):
            total = total + from_xy[k, n]
        from_z[pl.ds(z, 1), k] = total[None]
    for d in range(1, 8):
        start(from_z.at[z], from_z.at[z], 8, device(x, y, (z + d) & 7, c))
    more(GAPS[2])
    for t in range(3):
        level[t] = jnp.broadcast_to(energies[...], (16, N))[:, t * 128 : t * 128 + 128]
    wait(rsems.at[8], from_z.at[pl.ds(0, 7)])

    def finish(k):
        total = from_z[0, k]
        for n in range(1, 8):
            total = total + from_z[n, k]
        t = 16 * k + own
        r, g = lax.div(t, 3), lax.rem(t, 3)
        diagonal = iota((16, 128), 0) + 192 * c + 16 * r == iota((16, 128), 1) + 128 * g
        shown = (jnp.where(diagonal, level[g], 0.0) - total).astype(BF16)
        at = 36 * c + t
        fock_tiles[pl.ds(at, 1)] = shown[None]

        def tell(n, _):
            to = device((x + (n >> 3)) & 3, (y + ((n >> 1) & 3)) & 3, z, (c + n) & 1)
            start(fock_tiles.at[at], fock_tiles.at[at], 9, to)
            return 0

        lax.fori_loop(1, 32, tell, 0)

    finish(0)
    finish(1)

    @pl.when(own < 4)
    def _():
        finish(2)

    more(GAPS[3])

    block = lax.broadcasted_iota(jnp.int16, (32, 128), 1)
    taken = recv1.reshape(UNITS, 2 * D, 128)
    given = send2.reshape(UNITS, 2 * D, 128)

    def spot(u, i):
        g = 16 * u + i
        return g // 36, g % 12 * 32, g // 12 % 3 * 128

    for j in range(K):
        wait(rsems.at[j], all_but_one(recv1, IN_PARTS[j]))
        for u in range(IN_PARTS[j][0], IN_PARTS[j][0] + IN_PARTS[j][1]):
            got = turn_blocks([taken[u, 32 * b : 32 * b + 32, :] for b in range(16)], block)
            for i in range(16):
                k, row, lane = spot(u, i)
                if k < K:
                    mats[k, row : row + 32, lane : lane + 128] = got[i]
        held = mats[j]
        outs[j] = (dot(held, turn[...]) - dot_t(turn_t[...], held)).astype(BF16)

    @pl.when(own < 4)
    def _():
        wait(rsems.at[9], fock_tiles.at[pl.ds(0, 69)])

    @pl.when(own >= 4)
    def _():
        wait(rsems.at[9], fock_tiles.at[pl.ds(0, 70)])

    for t in range(2 * TILES):
        fock[t // 3 * 16 : t // 3 * 16 + 16, t % 3 * 128 : t % 3 * 128 + 128] = fock_tiles[t]
    fock_p[...] = dot_t(dot(gather, fock[...]).astype(BF16), gather).astype(BF16)

    for j in range(K):
        anti = outs[j]
        both = dot(fock_p[...], anti) + dot_t(anti, fock_p[...])
        slope = (factor[...] * both).astype(BF16)
        outs[j] = dot(slope, turn_t[...]).astype(BF16)
        for u in range(OUT_PARTS[j][0], OUT_PARTS[j][0] + OUT_PARTS[j][1]):
            pieces = []
            for i in range(16):
                k, row, lane = spot(u, i)
                pieces.append(outs[k, row : row + 32, lane : lane + 128] if k < K else jnp.zeros((32, 128), BF16))
            got = turn_blocks(pieces, block)
            for b in range(16):
                given[u, 32 * b : 32 * b + 32, :] = got[b]
        ship(1, D, OUT_PARTS[j], send2, recv2, 3 + j)
    recv2[:, pl.ds(me, 1)] = send2[:, pl.ds(me, 1)]

    taken = recv2.reshape(UNITS, 2 * D, 128)
    for j in range(K):
        wait(rsems.at[3 + j], all_but_one(recv2, OUT_PARTS[j]))
        for u in range(OUT_PARTS[j][0], OUT_PARTS[j][0] + OUT_PARTS[j][1]):
            turned = dot(dot_t(eye, taken[u]).astype(BF16), mix[...])
            for i in range(2):
                zs[i, 128 * u : 128 * u + 128, :] = turned[:, i * D : (i + 1) * D]
    for h in range(0, BB, 2 * B):
        rows = []
        for t in range(0, 2 * B, 8):
            p, g = (h + t) // B, ((h + t) % B) // 8
            pieces = []
            for j in range(K):
                at = ((j * 3 + g) * 12 + p // 2) * 8
                pieces.append(zs[p % 2, at : at + 8, :])
            rows.append(jnp.concatenate(pieces, axis=1))
        out[h : h + 2 * B] = jnp.concatenate(rows, axis=0).astype(BF16).reshape(2 * B, 2, N)

    for j in range(K):
        wait(sems.at[j], all_but_one(send1, IN_PARTS[j]))
        wait(sems.at[3 + j], all_but_one(send2, OUT_PARTS[j]))
    wait(sems.at[6], from_core)
    wait(sems.at[8], from_z.at[pl.ds(0, 7)])

    @pl.when(own < 4)
    def _():
        wait(sems.at[7], half.at[pl.ds(0, 33)])
        wait(sems.at[9], send1.at[pl.ds(0, 3), pl.ds(0, 248)])

    @pl.when(own >= 4)
    def _():
        wait(sems.at[7], half.at[pl.ds(0, 34)])
        wait(sems.at[9], send1.at[pl.ds(0, 2), pl.ds(0, 248)])


def shards(amplitudes, prev_slope, cholesky_vectors, energies, occupations):
    vmem = pl.BlockSpec(memory_space=pltpu.VMEM)
    whole = pl.BlockSpec(memory_space=pl.ANY)
    slope = pl.pallas_call(
        kernel,
        out_shape=jax.ShapeDtypeStruct((BB, 2, N), BF16),
        in_specs=[whole] * 3 + [vmem] * 2,
        out_specs=vmem,
        scratch_shapes=[
            pltpu.VMEM((BB, 2, N), BF16),
            pltpu.VMEM((BB, 2, N), BF16),
            pltpu.VMEM((144 * B, N), BF16),
            pltpu.VMEM((2, UNITS * 128, D), F32),
            pltpu.VMEM((512, 512), BF16),
            pltpu.VMEM((512, 512), BF16),
            pltpu.VMEM((UNITS, D, 2, 128), BF16),
            pltpu.VMEM((UNITS, D, 2, 128), BF16),
            pltpu.VMEM((UNITS, D, 2, 128), BF16),
            pltpu.VMEM((UNITS, D, 2, 128), BF16),
            pltpu.VMEM((K, N, N), BF16),
            pltpu.VMEM((K, N, N), BF16),
            pltpu.VMEM((N, N), F32),
            pltpu.VMEM((N, N), F32),
            pltpu.VMEM((TILES, 16, 128), F32),
            pltpu.VMEM((192, N), F32),
            pltpu.VMEM((3, 16, 16, 128), F32),
            pltpu.VMEM((8, 3, 16, 128), F32),
            pltpu.VMEM((3, 16, 128), F32),
            pltpu.VMEM((2 * TILES, 16, 128), BF16),
            pltpu.VMEM((N, N), BF16),
            pltpu.VMEM((N, N), BF16),
            pltpu.VMEM((N, N), F32),
            pltpu.VMEM((N, N), BF16),
            pltpu.VMEM((N, N), BF16),
            pltpu.SemaphoreType.REGULAR,
            pltpu.SemaphoreType.DMA((3,)),
            pltpu.SemaphoreType.DMA((10,)),
            pltpu.SemaphoreType.DMA((10,)),
        ],
        compiler_params=pltpu.CompilerParams(
            collective_id=0, has_side_effects=True, vmem_limit_bytes=56 << 20
        ),
    )(
        amplitudes.reshape(BB, 2, N),
        prev_slope.reshape(BB, 2, N),
        cholesky_vectors.reshape(-1, N),
        energies,
        occupations,
    )
    return slope.reshape(B, B, 2, N)


def solution(mesh):
    in_specs = (P("pa", "pb", None, None), P("pa", "pb", None, None), P("pb", "pa", None), P(), P())
    out_specs = P("pa", "pb", None, None)
    return jax.shard_map(shards, mesh=mesh, in_specs=in_specs, out_specs=out_specs, check_vma=False)
```

```python
import jax
import jax.numpy as jnp
from jax import lax
from jax.experimental import pallas as pl
from jax.experimental.pallas import tpu as pltpu
from jax.sharding import PartitionSpec as P

N = 384
B = 24
K = 3
BB = B * B
D = 256
UNITS = 7
F32 = jnp.float32
BF16 = jnp.bfloat16
MESH = pl.DeviceIdType.MESH
IN_PARTS = ((0, 3), (3, 2), (5, 2))
OUT_PARTS = ((0, 2), (2, 2), (4, 3))
GAPS = (255, 255, 255, 0)
TILES = 48
UPPER = ((0, 0), (0, 1), (0, 2), (1, 1), (1, 2), (2, 2))


def place():
    pa = lax.axis_index("pa")
    pb = lax.axis_index("pb")
    return pa >> 2, (pb >> 1) & 3, ((pb >> 3) << 2) | (pa & 3), pb & 1


def device(x, y, z, c):
    return (x << 2) | (z & 3), ((z >> 2) << 3) | (y << 1) | c


def partner(j):
    x, y, z, c = place()
    return device((x + (j >> 6)) & 3, (y + ((j >> 4) & 3)) & 3, (z + ((j >> 1) & 7)) & 7, (c + j) & 1)


def iota(shape, axis):
    return lax.broadcasted_iota(jnp.int32, shape, axis)


def one_hot(mask):
    return jnp.where(mask, 1.0, 0.0).astype(BF16)


def dot(a, b):
    return jnp.dot(a, b, preferred_element_type=F32)


def dot_t(a, b):
    return lax.dot_general(a, b, (((1,), (1,)), ((), ())), preferred_element_type=F32)


def row_home(rho):
    return ((rho >> 1) & 15) * B + (rho >> 5) * 2 + (rho & 1)


def lane_home(kappa):
    return ((kappa >> 3) & 15) * B + (kappa >> 7) * 8 + (kappa & 7)


def turn_blocks(xs, lane):
    xs = list(xs)
    for w in (1, 2, 4, 8):
        high = (lane & (8 * w)) != 0
        for i in range(16):
            if i & w == 0:
                a, b = xs[i], xs[i + w]
                xs[i] = jnp.where(high, pltpu.roll(b, 8 * w, 1), a)
                xs[i + w] = jnp.where(high, b, pltpu.roll(a, 128 - 8 * w, 1))
    return xs


def kernel(amp_hbm, prev_hbm, chol_hbm, energies, occ, out,
           amp, prev, chol, zs, mix, mix_t, send1, recv1, send2, recv2, mats, outs, holes,
           partial, half, from_core, from_xy, from_z, fock_tiles, fock, fock_p, factor, turn, turn_t,
           greet, loads, sems, rsems):
    x, y, z, c = place()
    me_a, me_b = device(x, y, z, c)
    me = (me_b << 4) | me_a

    load_amp = pltpu.make_async_copy(amp_hbm, amp, loads.at[0])
    load_prev = pltpu.make_async_copy(prev_hbm, prev, loads.at[1])
    load_chol = pltpu.make_async_copy(chol_hbm, chol, loads.at[2])
    load_chol.start()
    load_amp.start()
    load_prev.start()

    barrier = pltpu.get_barrier_semaphore()
    column = [device(x, y, (z + d) & 7, c ^ e) for d in range(8) for e in range(2) if d or e]
    plane = [device((x + d) & 3, (y + e) & 3, z, c) for d in range(4) for e in range(4) if d or e]
    for where in column + plane:
        pl.semaphore_signal(barrier, inc=1, device_id=where, device_id_type=MESH)

    def start(source, target, stage, where):
        pltpu.make_async_remote_copy(
            source, target, sems.at[stage], rsems.at[stage], device_id=where, device_id_type=MESH
        ).start()

    def wait(sem, like):
        pltpu.make_async_copy(like, like, sem).wait()

    def ship(lo, hi, part, source, target, stage):
        units = pl.ds(part[0], part[1])

        def step(j, _):
            qa, qb = partner(j)
            start(source.at[units, (qb << 4) | qa], target.at[units, me], stage, (qa, qb))
            return 0

        lax.fori_loop(lo, hi, step, 0)

    queue = [(j, n) for j in range(K) for n in range(1, D)]
    sent = [0]

    def more(count):
        todo = queue[sent[0] : sent[0] + count]
        sent[0] += count
        for j in range(K):
            ns = [n for k, n in todo if k == j]
            if ns:
                ship(ns[0], ns[-1] + 1, IN_PARTS[j], send1, recv1, j)

    def all_but_one(buf, part):
        return buf.at[pl.ds(part[0], part[1]), pl.ds(0, D - 1)]

    r, q = iota((512, 512), 0), iota((512, 512), 1)
    mix[...] = one_hot((r >> 1) + (r & 1) * D == q)
    mix_t[...] = one_hot((q >> 1) + (q & 1) * D == r)
    eye = one_hot(iota((128, 128), 0) == iota((128, 128), 1))

    spread = jnp.broadcast_to(occ[...], (128, N))
    upright = jnp.transpose(spread)
    partial[:, 0:128] = upright
    hole = 1.0 - 2.0 * partial[pl.ds(pl.multiple_of(me_a * B, 8), B), 0:128]
    for i in range(16):
        for t in range(3):
            holes[i * B : (i + 1) * B, t * 128 : t * 128 + 128] = hole
    load_chol.wait()
    partial[...] = jnp.zeros((N, N), F32)

    def rank_rows(i, _):
        rows = chol[pl.ds(pl.multiple_of(i * 3 * N, N), 3 * N), :]
        weighted = jnp.concatenate(
            [(rows[t * N : (t + 1) * N].astype(F32) * holes[...]).astype(BF16) for t in range(3)], axis=0
        )
        partial[...] += lax.dot_general(
            weighted, rows, (((0,), (0,)), ((), ())), preferred_element_type=F32
        )
        return 0

    lax.fori_loop(0, 3, rank_rows, 0)

    pl.semaphore_wait(barrier, len(column + plane))
    for where in plane:
        pl.semaphore_signal(greet, inc=1, device_id=where, device_id_type=MESH)
    for n, (r, g) in enumerate(UPPER):
        theirs = partial.at[pl.ds(pl.multiple_of(128 * r + 64 * (1 - c), 64), 64), pl.ds(128 * g, 128)]
        start(theirs, from_core.at[n], 6, device(x, y, z, 1 - c))
    load_amp.wait()
    load_prev.wait()
    for h in range(0, BB, 3 * B):
        s = amp[h : h + 3 * B].astype(F32) + 0.5 * prev[h : h + 3 * B].astype(F32)
        s = s.reshape(3 * B, 2 * N)
        for t in range(0, 3 * B, 8):
            p, g = (h + t) // B, ((h + t) % B) // 8
            for j in range(K):
                at = ((j * 3 + g) * 12 + p // 2) * 8
                zs[p % 2, at : at + 8, :] = s[t : t + 8, j * D : (j + 1) * D]
    for i in range(2):
        zs[i, 3 * BB // 2 :, :] = jnp.zeros((32, D), F32)
    folded = send1.reshape(UNITS, 2 * D, 128)
    for u in range(UNITS):
        pair = jnp.concatenate([zs[i, 128 * u : 128 * u + 128, :] for i in range(2)], axis=1).astype(BF16)
        folded[u] = dot_t(mix[...], pair).astype(BF16)
    recv1[:, pl.ds(me, 1)] = send1[:, pl.ds(me, 1)]

    wait(rsems.at[6], from_core)
    for n, (r, g) in enumerate(UPPER):
        ours = partial[pl.ds(pl.multiple_of(128 * r + 64 * c, 64), 64), g * 128 : g * 128 + 128] + from_core[n]
        for e in range(8):
            half[8 * n + e] = ours[8 * e : 8 * e + 8]
    own = (x << 2) | y

    def scatter(t, _):
        o = t & 15

        @pl.when(o != own)
        def _():
            start(half.at[t], from_xy.at[t >> 4, own], 7, device(o >> 2, o & 3, z, c))

        return 0

    lax.fori_loop(0, TILES, scatter, 0)
    pl.semaphore_wait(greet, len(plane))
    more(GAPS[0])
    rho, nat = iota((N, N), 0), iota((N, N), 1)
    home = row_home(rho)
    gather = one_hot(home == nat)
    turn_t[...] = one_hot(home == lane_home(nat))
    turn[...] = one_hot(lane_home(rho) == row_home(nat))
    left = spread
    order = jnp.zeros((128, N), F32)
    for _ in range(3):
        piece = left.astype(BF16)
        left = left - piece.astype(F32)
        order = order + dot_t(piece, gather)
    upright = jnp.transpose(order)
    for t in range(3):
        lanes = slice(t * 128, t * 128 + 128)
        factor[:, lanes] = -(1.0 - upright - order[0:1, lanes])

    more(GAPS[1])

    wait(rsems.at[7], from_xy.at[pl.ds(0, 3), pl.ds(0, 15)])
    for k in range(3):
        from_xy[k, pl.ds(own, 1)] = half[pl.ds(16 * k + own, 1)]
    for k in range(3):
        total = from_xy[k, 0]
        for n in range(1, 16):
            total = total + from_xy[k, n]
        from_z[pl.ds(z, 1), k] = total[None]
    for d in range(1, 8):
        start(from_z.at[z], from_z.at[z], 8, device(x, y, (z + d) & 7, c))
    more(GAPS[2])
    wait(rsems.at[8], from_z.at[pl.ds(0, 7)])

    def finish(k):
        total = from_z[0, k]
        for n in range(1, 8):
            total = total + from_z[n, k]
        at = TILES * c + 16 * k + own
        fock_tiles[pl.ds(at, 1)] = total[None]

        def tell(n, _):
            to = device((x + (n >> 3)) & 3, (y + ((n >> 1) & 3)) & 3, z, (c + n) & 1)
            start(fock_tiles.at[at], fock_tiles.at[at], 9, to)
            return 0

        lax.fori_loop(1, 32, tell, 0)

    for k in range(3):
        finish(k)

    more(GAPS[3])

    block = lax.broadcasted_iota(jnp.int16, (32, 128), 1)
    taken = recv1.reshape(UNITS, 2 * D, 128)
    given = send2.reshape(UNITS, 2 * D, 128)

    def spot(u, i):
        g = 16 * u + i
        return g // 36, g % 12 * 32, g // 12 % 3 * 128

    for j in range(K):
        wait(rsems.at[j], all_but_one(recv1, IN_PARTS[j]))
        for u in range(IN_PARTS[j][0], IN_PARTS[j][0] + IN_PARTS[j][1]):
            got = turn_blocks([taken[u, 32 * b : 32 * b + 32, :] for b in range(16)], block)
            for i in range(16):
                k, row, lane = spot(u, i)
                if k < K:
                    mats[k, row : row + 32, lane : lane + 128] = got[i]
        held = mats[j]
        outs[j] = (dot(held, turn[...]) - dot_t(turn_t[...], held)).astype(BF16)

    wait(rsems.at[9], fock_tiles.at[pl.ds(0, 2 * TILES - 3)])
    level = jnp.broadcast_to(energies[...], (128, N))
    diagonal = iota((128, 128), 0) == iota((128, 128), 1)
    for n, (r, g) in enumerate(UPPER):
        total = jnp.concatenate([fock_tiles[TILES * e + 8 * n + d] for e in range(2) for d in range(8)], axis=0)
        rows, lanes = slice(r * 128, r * 128 + 128), slice(g * 128, g * 128 + 128)
        if r == g:
            fock[rows, lanes] = (jnp.where(diagonal, level[:, lanes], 0.0) - total).astype(BF16)
        else:
            fock[rows, lanes] = (0.0 - total).astype(BF16)
            fock[lanes, rows] = (0.0 - jnp.transpose(total)).astype(BF16)
    fock_p[...] = dot_t(dot(gather, fock[...]).astype(BF16), gather).astype(BF16)

    for j in range(K):
        anti = outs[j]
        both = dot(fock_p[...], anti) + dot_t(anti, fock_p[...])
        slope = (factor[...] * both).astype(BF16)
        outs[j] = dot(slope, turn_t[...]).astype(BF16)
        for u in range(OUT_PARTS[j][0], OUT_PARTS[j][0] + OUT_PARTS[j][1]):
            pieces = []
            for i in range(16):
                k, row, lane = spot(u, i)
                pieces.append(outs[k, row : row + 32, lane : lane + 128] if k < K else jnp.zeros((32, 128), BF16))
            got = turn_blocks(pieces, block)
            for b in range(16):
                given[u, 32 * b : 32 * b + 32, :] = got[b]
        ship(1, D, OUT_PARTS[j], send2, recv2, 3 + j)
    recv2[:, pl.ds(me, 1)] = send2[:, pl.ds(me, 1)]

    taken = recv2.reshape(UNITS, 2 * D, 128)
    for j in range(K):
        wait(rsems.at[3 + j], all_but_one(recv2, OUT_PARTS[j]))
        for u in range(OUT_PARTS[j][0], OUT_PARTS[j][0] + OUT_PARTS[j][1]):
            turned = dot(dot_t(eye, taken[u]).astype(BF16), mix[...])
            for i in range(2):
                zs[i, 128 * u : 128 * u + 128, :] = turned[:, i * D : (i + 1) * D]
    for h in range(0, BB, 2 * B):
        rows = []
        for t in range(0, 2 * B, 8):
            p, g = (h + t) // B, ((h + t) % B) // 8
            pieces = []
            for j in range(K):
                at = ((j * 3 + g) * 12 + p // 2) * 8
                pieces.append(zs[p % 2, at : at + 8, :])
            rows.append(jnp.concatenate(pieces, axis=1))
        out[h : h + 2 * B] = jnp.concatenate(rows, axis=0).astype(BF16).reshape(2 * B, 2, N)

    for j in range(K):
        wait(sems.at[j], all_but_one(send1, IN_PARTS[j]))
        wait(sems.at[3 + j], all_but_one(send2, OUT_PARTS[j]))
    wait(sems.at[6], from_core)
    wait(sems.at[7], half.at[pl.ds(0, 45)])
    wait(sems.at[8], from_z.at[pl.ds(0, 7)])
    wait(sems.at[9], fock_tiles.at[pl.ds(0, 2 * TILES - 3)])


def shards(amplitudes, prev_slope, cholesky_vectors, energies, occupations):
    vmem = pl.BlockSpec(memory_space=pltpu.VMEM)
    whole = pl.BlockSpec(memory_space=pl.ANY)
    slope = pl.pallas_call(
        kernel,
        out_shape=jax.ShapeDtypeStruct((BB, 2, N), BF16),
        in_specs=[whole] * 3 + [vmem] * 2,
        out_specs=vmem,
        scratch_shapes=[
            pltpu.VMEM((BB, 2, N), BF16),
            pltpu.VMEM((BB, 2, N), BF16),
            pltpu.VMEM((144 * B, N), BF16),
            pltpu.VMEM((2, UNITS * 128, D), F32),
            pltpu.VMEM((512, 512), BF16),
            pltpu.VMEM((512, 512), BF16),
            pltpu.VMEM((UNITS, D, 2, 128), BF16),
            pltpu.VMEM((UNITS, D, 2, 128), BF16),
            pltpu.VMEM((UNITS, D, 2, 128), BF16),
            pltpu.VMEM((UNITS, D, 2, 128), BF16),
            pltpu.VMEM((K, N, N), BF16),
            pltpu.VMEM((K, N, N), BF16),
            pltpu.VMEM((N, N), F32),
            pltpu.VMEM((N, N), F32),
            pltpu.VMEM((TILES, 8, 128), F32),
            pltpu.VMEM((6, 64, 128), F32),
            pltpu.VMEM((3, 16, 8, 128), F32),
            pltpu.VMEM((8, 3, 8, 128), F32),
            pltpu.VMEM((2 * TILES, 8, 128), F32),
            pltpu.VMEM((N, N), BF16),
            pltpu.VMEM((N, N), BF16),
            pltpu.VMEM((N, N), F32),
            pltpu.VMEM((N, N), BF16),
            pltpu.VMEM((N, N), BF16),
            pltpu.SemaphoreType.REGULAR,
            pltpu.SemaphoreType.DMA((3,)),
            pltpu.SemaphoreType.DMA((10,)),
            pltpu.SemaphoreType.DMA((10,)),
        ],
        compiler_params=pltpu.CompilerParams(
            collective_id=0, has_side_effects=True, vmem_limit_bytes=56 << 20
        ),
    )(
        amplitudes.reshape(BB, 2, N),
        prev_slope.reshape(BB, 2, N),
        cholesky_vectors.reshape(-1, N),
        energies,
        occupations,
    )
    return slope.reshape(B, B, 2, N)


def solution(mesh):
    in_specs = (P("pa", "pb", None, None), P("pa", "pb", None, None), P("pb", "pa", None), P(), P())
    out_specs = P("pa", "pb", None, None)
    return jax.shard_map(shards, mesh=mesh, in_specs=in_specs, out_specs=out_specs, check_vma=False)
```
